32 devices in a mesh: dp: 4 (over z), row: 2 (over x), col: 4 (over y, core).
Axes of the slice: x: 2, y: 2, z: 4, core: 2. Of those that a mesh axis runs over, the one named last changes fastest.
Arguments:
- tokens: bfloat16 [4096, 1024], P('dp', ('col', 'row'))
- segment_ids: int32 [4096], P('dp'), may hold values from 0 to 15, never falling along the last dimension, each value on 1 to 2048 neighbouring positions
- out_grad: bfloat16 [4096, 1024], P('dp', ('col', 'row')), may hold values from -6 to 6
- qkv_weight: float32 [1024, 16, 3, 64], P(('col', 'dp'), 'row'), may hold values from -0.1875 to 0.1875
- qkv_first: float32 [1024, 16, 3, 64], P(('col', 'dp'), 'row')
- qkv_second: float32 [1024, 16, 3, 64], P(('col', 'dp'), 'row')
- out_weight: float32 [1024, 1024], P(('row', 'dp'), 'col'), may hold values from -1.5 to 1.5
- out_first: float32 [1024, 1024], P(('row', 'dp'), 'col')
- out_second: float32 [1024, 1024], P(('row', 'dp'), 'col')
- up_weight: float32 [1024, 4096], P('col', ('row', 'dp')), may hold values from -0.1875 to 0.1875
- up_first: float32 [1024, 4096], P('col', ('row', 'dp'))
- up_second: float32 [1024, 4096], P('col', ('row', 'dp'))
- down_weight: float32 [4096, 1024], P(('row', 'dp'), 'col'), may hold values from -0.09375 to 0.09375
- down_first: float32 [4096, 1024], P(('row', 'dp'), 'col')
- down_second: float32 [4096, 1024], P(('row', 'dp'), 'col')
- qkv_bias: float32 [16, 192], P(('row', 'col'), 'dp'), may hold values from -1.5 to 1.5
- qkv_bias_first: float32 [16, 192], P(('row', 'col'), 'dp')
- qkv_bias_second: float32 [16, 192], P(('row', 'col'), 'dp')
- up_bias: float32 [4096], P(('row', 'col', 'dp')), may hold values from -1.5 to 1.5
- up_bias_first: float32 [4096], P(('row', 'col', 'dp'))
- up_bias_second: float32 [4096], P(('row', 'col', 'dp'))
- norm_vectors: float32 [6, 1024], P(None, ('col', 'row', 'dp'))
- norm_first: float32 [6, 1024], P(None, ('col', 'row', 'dp'))
- norm_second: float32 [6, 1024], P(None, ('col', 'row', 'dp'))
Outputs:
- block_out: bfloat16 [4096, 1024], P('dp', ('col', 'row'))
- input_grad: float32 [4096, 1024], P('dp', ('col', 'row'))
- new_qkv_weight: float32 [1024, 16, 3, 64], P(('col', 'dp'), 'row')
- new_qkv_first: float32 [1024, 16, 3, 64], P(('col', 'dp'), 'row')
- new_qkv_second: float32 [1024, 16, 3, 64], P(('col', 'dp'), 'row')
- new_out_weight: float32 [1024, 1024], P(('row', 'dp'), 'col')
- new_out_first: float32 [1024, 1024], P(('row', 'dp'), 'col')
- new_out_second: float32 [1024, 1024], P(('row', 'dp'), 'col')
- new_up_weight: float32 [1024, 4096], P('col', ('row', 'dp'))
- new_up_first: float32 [1024, 4096], P('col', ('row', 'dp'))
- new_up_second: float32 [1024, 4096], P('col', ('row', 'dp'))
- new_down_weight: float32 [4096, 1024], P(('row', 'dp'), 'col')
- new_down_first: float32 [4096, 1024], P(('row', 'dp'), 'col')
- new_down_second: float32 [4096, 1024], P(('row', 'dp'), 'col')
- new_qkv_bias: float32 [16, 192], P(('row', 'col'), 'dp')
- new_qkv_bias_first: float32 [16, 192], P(('row', 'col'), 'dp')
- new_qkv_bias_second: float32 [16, 192], P(('row', 'col'), 'dp')
- new_up_bias: float32 [4096], P(('row', 'col', 'dp'))
- new_up_bias_first: float32 [4096], P(('row', 'col', 'dp'))
- new_up_bias_second: float32 [4096], P(('row', 'col', 'dp'))
- new_norm_vectors: float32 [6, 1024], P(None, ('col', 'row', 'dp'))
- new_norm_first: float32 [6, 1024], P(None, ('col', 'row', 'dp'))
- new_norm_second: float32 [6, 1024], P(None, ('col', 'row', 'dp'))
The draws below stay inside these ranges and needn't reach their ends.
Inputs may be any that keep to these rules, and one draw needn't show every extreme that they name: `segment_ids`: ids never fall along the tokens; each id covers 1 to 2048 consecutive tokens and one covers exactly 2048.
All inputs are finite; a program needn't handle non-finite values.
Results may differ from the reference program's by a relative error of at most 0.02.
Values may be sent and summed in bfloat16 or wider, within the bound.
A program may use at most 128 MiB of HBM per device.

```python
import math
import jax
import jax.numpy as jnp
import numpy as np
from jax import lax

D = 1024
H = 16
HD = 64
FF = 4096
SEQ = 512
SEQS = 2
STEP = 10
TOK_GRP = 1024
TOKENS = 4096
DOCS = 16
DOC_MAX = 2048
N_DP = 4


def moment_first(key, array_shape, grad_scale):
    return 0.11 * grad_scale * jax.random.normal(key, array_shape, jnp.float32)


def moment_second(key, array_shape, grad_scale):
    spread = jax.random.uniform(key, array_shape, jnp.float32, math.log(0.5), math.log(8.0))
    return 0.001 * grad_scale * grad_scale * jnp.exp(spread)


def draw_tokens(key, part):
    key = jax.random.fold_in(key, 1)
    ramp = jnp.arange(D, dtype=jnp.float32) / D
    noise = jax.random.normal(key, (TOKENS, D), jnp.float32)
    return (noise * (0.6 * jnp.exp(math.log(3.0) * ramp))).astype(jnp.bfloat16)


def draw_norm_vectors(key, part):
    key = jax.random.fold_in(key, 2)
    biases = jax.random.uniform(key, (6, D), jnp.float32, -0.5, 0.5)
    gains = jax.random.uniform(jax.random.fold_in(key, 7), (6, D), jnp.float32, 0.6, 1.4)
    picked = (jnp.arange(6) % 3 == 1)[:, None]
    return jnp.where(picked, gains, biases)


def draw_qkv_first(key, part):
    key = jax.random.fold_in(key, 11)
    return moment_first(key, (D, H, 3, HD), 0.7 * math.sqrt(TOKENS))


def draw_qkv_second(key, part):
    key = jax.random.fold_in(key, 12)
    return moment_second(key, (D, H, 3, HD), 0.7 * math.sqrt(TOKENS))


def draw_out_first(key, part):
    key = jax.random.fold_in(key, 13)
    return moment_first(key, (D, D), 0.1 * math.sqrt(TOKENS))


def draw_out_second(key, part):
    key = jax.random.fold_in(key, 14)
    return moment_second(key, (D, D), 0.1 * math.sqrt(TOKENS))


def draw_up_first(key, part):
    key = jax.random.fold_in(key, 15)
    return moment_first(key, (D, FF), 0.3 * math.sqrt(TOKENS))


def draw_up_second(key, part):
    key = jax.random.fold_in(key, 16)
    return moment_second(key, (D, FF), 0.3 * math.sqrt(TOKENS))


def draw_down_first(key, part):
    key = jax.random.fold_in(key, 17)
    return moment_first(key, (FF, D), 0.5 * math.sqrt(TOKENS))


def draw_down_second(key, part):
    key = jax.random.fold_in(key, 18)
    return moment_second(key, (FF, D), 0.5 * math.sqrt(TOKENS))


def draw_qkv_bias_first(key, part):
    key = jax.random.fold_in(key, 19)
    return moment_first(key, (H, 3 * HD), 0.6 * math.sqrt(TOKENS))


def draw_qkv_bias_second(key, part):
    key = jax.random.fold_in(key, 20)
    return moment_second(key, (H, 3 * HD), 0.6 * math.sqrt(TOKENS))


def draw_up_bias_first(key, part):
    key = jax.random.fold_in(key, 21)
    return moment_first(key, (FF,), 0.3 * math.sqrt(TOKENS))


def draw_up_bias_second(key, part):
    key = jax.random.fold_in(key, 22)
    return moment_second(key, (FF,), 0.3 * math.sqrt(TOKENS))


def draw_norm_first(key, part):
    key = jax.random.fold_in(key, 23)
    return moment_first(key, (6, D), 0.9 * math.sqrt(TOKENS))


def draw_norm_second(key, part):
    key = jax.random.fold_in(key, 24)
    return moment_second(key, (6, D), 0.9 * math.sqrt(TOKENS))


def block_scale(stream_key, extent, cuts, smallest, high):
    factor_of = 1.0
    for axis_at, shards_of in cuts:
        steps = jax.random.uniform(jax.random.fold_in(jax.random.fold_in(stream_key, 6), axis_at), (shards_of,), jnp.float32, smallest / len(cuts), high / len(cuts))
        factor_of = factor_of * jnp.repeat(jnp.exp(steps), extent[axis_at] // shards_of).reshape((-1,) + (1,) * (len(extent) - 1 - axis_at))
    return factor_of


def split_up(count, total, reach, skew):
    loads = [(1 << 20) // math.isqrt(grade ** skew) + 1 for grade in range(2, count + 1)]
    rest, holding = total - reach - (count - 1), [1] * (count - 1)
    while rest > 0:
        free = [i for i in range(count - 1) if holding[i] < reach]
        whole, budget = sum([loads[i] for i in free]), rest
        for i in free:
            more = min(reach - holding[i], max(1, budget * loads[i] // whole), rest)
            holding[i] = holding[i] + more
            rest = rest - more
    return np.array([reach] + holding)


def ragged_sizes(own_key, amount, total, reach, lean):
    if amount == 2:
        one = jax.random.randint(own_key, (), max(1, total - reach), min(reach, total - 1) + 1)
        return jnp.stack([one, total - one])
    sizes = jnp.asarray(split_up(amount, total, reach, lean), jnp.int32)
    pairs = (amount - 1) // 2
    source_of, receiver = sizes[1:1 + 2 * pairs:2], sizes[2:2 + 2 * pairs:2]
    room = jnp.minimum(source_of - 1, reach - receiver)
    shifted = jax.random.randint(jax.random.fold_in(own_key, 1), (pairs,), 0, 1 << 20) % (room + 1)
    sizes = sizes.at[1:1 + 2 * pairs:2].set(source_of - shifted).at[2:2 + 2 * pairs:2].set(receiver + shifted)
    return sizes[jax.random.permutation(jax.random.fold_in(own_key, 2), amount)]


def bell_draw(key, extent, width, limit, pieces=(), kind=jnp.bfloat16):
    drawn = jax.random.normal(key, extent, jnp.float32) * width
    if len(pieces) > 0:
        drawn = block_scale(key, extent, pieces, -0.22, 0.18) * drawn
    return jnp.clip(drawn, min=-limit, max=limit).astype(kind)


def setup_inputs(seed: int = 0) -> dict:
    splits = jax.random.split(jax.random.key(seed), 25)
    tokens = draw_tokens(jax.random.fold_in(splits[24], 71), 0)
    segment_ids = jnp.searchsorted(jnp.cumsum(ragged_sizes(splits[1], DOCS, TOKENS, DOC_MAX, 2)), jnp.arange(TOKENS), side="right").astype(jnp.int32)
    out_grad = bell_draw(splits[2], (TOKENS, D), 1.0, 6.0, ((0, 4), (1, 8)))
    qkv_weight = bell_draw(splits[3], (D, H, 3, HD), D ** -0.5, 0.1875, ((0, 16), (1, 2)), jnp.float32)
    qkv_first = draw_qkv_first(jax.random.fold_in(splits[24], 71), 0)
    qkv_second = draw_qkv_second(jax.random.fold_in(splits[24], 71), 0)
    out_weight = bell_draw(splits[6], (D, D), (D // 64) ** -0.5, 1.5, ((0, 8), (1, 4)), jnp.float32)
    out_first = draw_out_first(jax.random.fold_in(splits[24], 71), 0)
    out_second = draw_out_second(jax.random.fold_in(splits[24], 71), 0)
    up_weight = bell_draw(splits[9], (D, FF), D ** -0.5, 0.1875, ((0, 4), (1, 8)), jnp.float32)
    up_first = draw_up_first(jax.random.fold_in(splits[24], 71), 0)
    up_second = draw_up_second(jax.random.fold_in(splits[24], 71), 0)
    down_weight = bell_draw(splits[12], (FF, D), FF ** -0.5, 0.09375, ((0, 8), (1, 4)), jnp.float32)
    down_first = draw_down_first(jax.random.fold_in(splits[24], 71), 0)
    down_second = draw_down_second(jax.random.fold_in(splits[24], 71), 0)
    qkv_bias = bell_draw(splits[15], (H, 3 * HD), 0.3, 1.5, ((0, 8), (1, 4)), jnp.float32)
    qkv_bias_first = draw_qkv_bias_first(jax.random.fold_in(splits[24], 71), 0)
    qkv_bias_second = draw_qkv_bias_second(jax.random.fold_in(splits[24], 71), 0)
    up_bias = bell_draw(splits[18], (FF,), 0.3, 1.5, ((0, 32),), jnp.float32)
    up_bias_first = draw_up_bias_first(jax.random.fold_in(splits[24], 71), 0)
    up_bias_second = draw_up_bias_second(jax.random.fold_in(splits[24], 71), 0)
    norm_vectors = draw_norm_vectors(jax.random.fold_in(splits[24], 71), 0)
    norm_first = draw_norm_first(jax.random.fold_in(splits[24], 71), 0)
    norm_second = draw_norm_second(jax.random.fold_in(splits[24], 71), 0)
    return {"tokens": tokens, "segment_ids": segment_ids, "out_grad": out_grad, "qkv_weight": qkv_weight, "qkv_first": qkv_first, "qkv_second": qkv_second, "out_weight": out_weight, "out_first": out_first, "out_second": out_second, "up_weight": up_weight, "up_first": up_first, "up_second": up_second, "down_weight": down_weight, "down_first": down_first, "down_second": down_second, "qkv_bias": qkv_bias, "qkv_bias_first": qkv_bias_first, "qkv_bias_second": qkv_bias_second, "up_bias": up_bias, "up_bias_first": up_bias_first, "up_bias_second": up_bias_second, "norm_vectors": norm_vectors, "norm_first": norm_first, "norm_second": norm_second}


EPS_NORM = 1e-05
BETA_ONE = 0.9
BETA_TWO = 0.999
EPS_ADAM = 1e-08
NEG_FILL = -1000000000.0
RATES = (0.05, 0.4, 0.05, 0.05, 0.3, 0.3, 0.5)
DECAYS = (0.01, 0.01, 0.01, 0.01, 0.0, 0.0, 0.0)

@jax.custom_vjp
def low(v):
    return lax.optimization_barrier(v.astype(jnp.bfloat16)).astype(jnp.float32)

@jax.custom_vjp
def low_back(v):
    return v

def low_keep(v):
    return (low(v), None)

def low_pass(kept, grad):
    return (grad,)

def back_keep(v):
    return (v, None)

def back_low(kept, grad):
    return (low(grad),)
low.defvjp(low_keep, low_pass)
low_back.defvjp(back_keep, back_low)

def matmul(left_side, right_side):
    return jnp.dot(left_side, right_side, precision=lax.Precision.HIGHEST, preferred_element_type=jnp.float32)

def layer_norm(residual, norm_gain, norm_shift):
    mean_row = lax.optimization_barrier(jnp.mean(residual, axis=-1, keepdims=True))
    square_row = lax.optimization_barrier(jnp.mean(residual * residual, axis=-1, keepdims=True))
    scale_row = lax.rsqrt(square_row - mean_row * mean_row + EPS_NORM)
    return (residual - mean_row) * scale_row * norm_gain + norm_shift

def group_forward(params, token_rows, segment_rows):
    w_qkv, w_out, w_up, w_down, b_qkv, b_up, vectors = params
    row_count = token_rows.shape[0]
    score_scale = 1.0 / math.sqrt(HD)
    qkv_all = low_back(matmul(token_rows, w_qkv.reshape(D, H * 3 * HD))) + b_qkv.reshape(H * 3 * HD)
    qkv_all = low(qkv_all).reshape(SEQS, SEQ, H, 3, HD)
    queries = qkv_all[:, :, :, 0]
    key_rows = qkv_all[:, :, :, 1]
    value_rows = qkv_all[:, :, :, 2]
    raw_scores = jnp.einsum('sqhd,skhd->shqk', queries, key_rows, precision=lax.Precision.HIGHEST) * score_scale
    raw_scores = low_back(raw_scores)
    seg_rows = segment_rows.reshape(SEQS, SEQ)
    same_doc = seg_rows[:, None, :, None] == seg_rows[:, None, None, :]
    masked = jnp.where(same_doc, raw_scores, NEG_FILL)
    row_peak = lax.optimization_barrier(jnp.max(masked, axis=-1, keepdims=True))
    exp_scores = jnp.exp(masked - row_peak)
    soft_weights = exp_scores / lax.optimization_barrier(jnp.sum(exp_scores, axis=-1, keepdims=True))
    attended = jnp.einsum('shqk,skhd->sqhd', low(soft_weights), value_rows, precision=lax.Precision.HIGHEST)
    attended = low(low_back(attended)).reshape(row_count, D)
    residual_one = token_rows + low_back(matmul(attended, w_out)) + vectors[0]
    hidden_one = layer_norm(residual_one, vectors[1], vectors[2])
    pre_act = low_back(matmul(low(hidden_one), w_up)) + b_up
    activation = low(jax.nn.gelu(pre_act, approximate=False))
    residual_two = hidden_one + low_back(matmul(activation, w_down)) + vectors[3]
    return layer_norm(residual_two, vectors[4], vectors[5])

def reference(tokens, segment_ids, out_grad, qkv_weight, qkv_first, qkv_second, out_weight, out_first, out_second, up_weight, up_first, up_second, down_weight, down_first, down_second, qkv_bias, qkv_bias_first, qkv_bias_second, up_bias, up_bias_first, up_bias_second, norm_vectors, norm_first, norm_second):
    masters = (qkv_weight, out_weight, up_weight, down_weight, qkv_bias, up_bias, norm_vectors)
    firsts = (qkv_first, out_first, up_first, down_first, qkv_bias_first, up_bias_first, norm_first)
    seconds = (qkv_second, out_second, up_second, down_second, qkv_bias_second, up_bias_second, norm_second)
    token_groups = tokens.astype(jnp.float32).reshape(N_DP, TOK_GRP, D)
    segment_groups = segment_ids.reshape(N_DP, TOK_GRP)
    group_step = jax.checkpoint(group_forward)

    def forward(token_all, params):
        rounded = tuple((low(param) for param in params))

        def scan_body(carry, item_pair):
            return (carry, group_step(rounded, item_pair[0], item_pair[1]))
        carry_out, layer_outputs = lax.scan(scan_body, jnp.zeros((), jnp.float32), (token_all, segment_groups))
        return layer_outputs
    layer_outputs, pullback = jax.vjp(forward, token_groups, masters)
    input_grads, gradients = pullback(out_grad.astype(jnp.float32).reshape(N_DP, TOK_GRP, D))
    correct_one = 1.0 - BETA_ONE ** STEP
    correct_two = 1.0 - BETA_TWO ** STEP
    results = []
    for master, first_old, second_old, gradient, step_rate, decay_rate in zip(masters, firsts, seconds, gradients, RATES, DECAYS):
        new_first = BETA_ONE * first_old + (1.0 - BETA_ONE) * gradient
        new_second = BETA_TWO * second_old + (1.0 - BETA_TWO) * gradient * gradient
        direction = new_first / correct_one / (jnp.sqrt(new_second / correct_two) + EPS_ADAM)
        results.append(master - step_rate * (direction + decay_rate * master))
        results.append(new_first)
        results.append(new_second)
    block_out = layer_outputs.reshape(TOKENS, D).astype(jnp.bfloat16)
    input_grad = input_grads.reshape(TOKENS, D)
    return (block_out, input_grad, results[0], results[1], results[2], results[3], results[4], results[5], results[6], results[7], results[8], results[9], results[10], results[11], results[12], results[13], results[14], results[15], results[16], results[17], results[18], results[19], results[20])
```

```python
import math

import jax
import jax.numpy as jnp
from jax import lax
from jax.sharding import PartitionSpec as P

D = 1024
HD = 64
SEQ = 512
STEP = 10


EPS_NORM = 1e-05
BETA_ONE = 0.9
BETA_TWO = 0.999
EPS_ADAM = 1e-08
NEG_FILL = -1000000000.0
RATES = (0.05, 0.4, 0.05, 0.05, 0.3, 0.3, 0.5)
DECAYS = (0.01, 0.01, 0.01, 0.01, 0.0, 0.0, 0.0)


GROUP = ("col", "row")


def group_gather(block):
    return lax.all_gather(block, GROUP, axis=0, tiled=True)


def feature_gather(block):
    return lax.all_gather(block, GROUP, axis=1, tiled=True)


def group_scatter(partial_terms):
    return lax.psum_scatter(
        partial_terms.astype(jnp.bfloat16), GROUP, scatter_dimension=0, tiled=True
    ).astype(jnp.float32)


def feature_scatter(partial_terms):
    return lax.psum_scatter(
        partial_terms.astype(jnp.bfloat16), GROUP, scatter_dimension=1, tiled=True
    ).astype(jnp.float32)


def to_tokens(block):
    return lax.all_to_all(block, GROUP, split_axis=0, concat_axis=1, tiled=True)


def to_features(block):
    return lax.all_to_all(block, GROUP, split_axis=1, concat_axis=0, tiled=True)


def contract_rows(left_side, right_side):
    return lax.dot_general(
        left_side, right_side, (((0,), (0,)), ((), ())), preferred_element_type=jnp.float32
    )


def contract_cols(left_side, right_side):
    return lax.dot_general(
        left_side, right_side, (((1,), (1,)), ((), ())), preferred_element_type=jnp.float32
    )


def gelu_exact(values_in):
    return jax.nn.gelu(values_in, approximate=False)


def norm_forward(residual, norm_gain, norm_shift):
    mean_row = jnp.sum(residual, axis=1, keepdims=True) / D
    square_row = jnp.sum(residual * residual, axis=1, keepdims=True) / D
    scale_row = lax.rsqrt(square_row - mean_row * mean_row + EPS_NORM)
    normed = (residual - mean_row) * scale_row
    return (normed * norm_gain + norm_shift, normed, scale_row)


def norm_backward(grad_out, norm_gain, normed, scale_row):
    grad_normed = grad_out * norm_gain
    sum_plain = jnp.sum(grad_normed, axis=1, keepdims=True)
    sum_cross = jnp.sum(grad_normed * normed, axis=1, keepdims=True)
    grad_resid = scale_row * (grad_normed - sum_plain / D - normed * (sum_cross / D))
    return (grad_resid, jnp.sum(grad_out * normed, axis=0), jnp.sum(grad_out, axis=0))


def masked_scores(queries, key_rows, same_doc):
    raw_scores = jnp.einsum(
        "sqhd,skhd->shqk", queries, key_rows, preferred_element_type=jnp.float32
    ) * (1.0 / math.sqrt(HD))
    return jnp.where(same_doc, raw_scores, NEG_FILL)


def shards(
    tokens,
    segment_ids,
    out_grad,
    qkv_weight,
    qkv_first,
    qkv_second,
    out_weight,
    out_first,
    out_second,
    up_weight,
    up_first,
    up_second,
    down_weight,
    down_first,
    down_second,
    qkv_bias,
    qkv_bias_first,
    qkv_bias_second,
    up_bias,
    up_bias_first,
    up_bias_second,
    norm_vectors,
    norm_first,
    norm_second,
):
    masters = (qkv_weight, out_weight, up_weight, down_weight, qkv_bias, up_bias, norm_vectors)
    firsts = (qkv_first, out_first, up_first, down_first, qkv_bias_first, up_bias_first, norm_first)
    seconds = (
        qkv_second,
        out_second,
        up_second,
        down_second,
        qkv_bias_second,
        up_bias_second,
        norm_second,
    )
    bf16 = jnp.bfloat16
    f32 = jnp.float32
    n_dp, n_row, n_col = (lax.axis_size(name) for name in ("dp", "row", "col"))
    at_dp, at_row, at_col = (lax.axis_index(name) for name in ("dp", "row", "col"))
    at_group = at_col * n_row + at_row
    tok_count = tokens.shape[0]
    own_tok = tok_count // (n_row * n_col)
    seq_count = tok_count // SEQ
    score_scale = 1.0 / math.sqrt(HD)
    qkv_rows, heads_row = qkv_weight.shape[:2]
    heads_local = heads_row // n_col
    width = heads_local * 3 * HD
    feats = heads_local * HD
    d_col = D // n_col
    ff_own = up_weight.shape[1] // n_col
    ff_local = ff_own * n_dp
    w_qkv = lax.all_gather(
        lax.all_to_all(
            qkv_weight.astype(bf16).reshape(qkv_rows, n_col, width), "col", 1, 0, tiled=True
        ).reshape(n_col, qkv_rows, width),
        "dp",
        axis=1,
    ).reshape(D, width)
    w_out = (
        lax.all_to_all(
            lax.all_gather(out_weight.astype(bf16), "dp", axis=0, tiled=True).reshape(
                n_col, feats, d_col
            ),
            "col",
            0,
            2,
            tiled=True,
        )
    ).reshape(feats, D)
    w_up = lax.all_gather(
        lax.all_to_all(up_weight.astype(bf16).T, "col", 0, 1, tiled=True), "dp", axis=0, tiled=True
    )
    w_down = lax.all_gather(
        lax.all_to_all(down_weight.astype(bf16), "col", 0, 1, tiled=True), "dp", axis=0, tiled=True
    )
    n_vec = norm_vectors.shape[1]
    small = lax.all_gather(
        jnp.concatenate(
            (norm_vectors.reshape(-1), qkv_bias.reshape(-1), up_bias.reshape(-1))
        ).astype(bf16),
        ("col", "row", "dp"),
        axis=0,
    ).astype(f32)
    vec_size, qb_size = norm_vectors.size, qkv_bias.size
    vector_rows = (
        small[:, :vec_size].reshape(-1, 6, n_vec).transpose(1, 0, 2).reshape(6, D)
    )
    small_group = small.reshape(n_col, n_row, n_dp, -1)
    qb_all = lax.dynamic_index_in_dim(
        small_group[..., vec_size : vec_size + qb_size].reshape(n_col * n_row, n_dp, -1),
        at_group,
        0,
        keepdims=False,
    )
    b_qkv = qb_all.reshape(n_dp, heads_local, -1).transpose(1, 0, 2).reshape(-1)
    ub_all = lax.dynamic_index_in_dim(
        small_group[..., vec_size + qb_size :], at_row, 1, keepdims=False
    ).reshape(n_dp, n_col, ff_own)
    b_up = lax.dynamic_index_in_dim(ub_all, at_col, 1, keepdims=False).reshape(-1)

    seg_rows = segment_ids.reshape(seq_count, SEQ)
    same_doc = seg_rows[:, None, :, None] == seg_rows[:, None, None, :]
    token_rows = feature_gather(tokens)
    own_tokens = lax.dynamic_slice_in_dim(token_rows, at_group * own_tok, own_tok, 0)
    own_out_grad = to_tokens(out_grad).astype(f32)
    qkv_local = jnp.dot(token_rows, w_qkv, preferred_element_type=f32) + b_qkv
    qkv_low = qkv_local.astype(bf16).reshape(seq_count, SEQ, heads_local, 3, HD)
    queries = qkv_low[:, :, :, 0]
    key_rows = qkv_low[:, :, :, 1]
    value_rows = qkv_low[:, :, :, 2]
    scores = masked_scores(queries, key_rows, same_doc)
    row_peak = jnp.max(scores, axis=-1, keepdims=True)
    exp_scores = jnp.exp(scores - row_peak)
    row_total = jnp.sum(exp_scores, axis=-1, keepdims=True)
    log_total = row_peak + jnp.log(row_total)
    soft_low = (exp_scores / row_total).astype(bf16)
    attended = (
        jnp.einsum("shqk,skhd->sqhd", soft_low, value_rows, preferred_element_type=f32)
        .reshape(tok_count, feats)
        .astype(bf16)
    )
    residual_one = (
        own_tokens.astype(f32)
        + group_scatter(jnp.dot(attended, w_out, preferred_element_type=f32))
        + vector_rows[0]
    )
    hidden_one, normed_one, scale_one = norm_forward(residual_one, vector_rows[1], vector_rows[2])
    hidden_rows = group_gather(hidden_one.astype(bf16))
    pre_act = contract_cols(hidden_rows, w_up) + b_up
    act_rows = gelu_exact(pre_act).astype(bf16)
    residual_two = (
        hidden_one
        + group_scatter(jnp.dot(act_rows, w_down, preferred_element_type=f32))
        + vector_rows[3]
    )
    output_rows, normed_two, scale_two = norm_forward(residual_two, vector_rows[4], vector_rows[5])
    block_out = to_features(output_rows.astype(bf16))
    grad_two, grad_gain_two, grad_shift_two = norm_backward(
        own_out_grad, vector_rows[4], normed_two, scale_two
    )
    grad_down_bias = jnp.sum(grad_two, axis=0)
    grad_two_rows = group_gather(grad_two.astype(bf16))
    grad_act = contract_cols(grad_two_rows, w_down)
    gelu_value, gelu_pull = jax.vjp(gelu_exact, pre_act)
    grad_pre = gelu_pull(grad_act)[0]
    grad_up_bias = jnp.sum(grad_pre, axis=0)
    grad_pre_low = grad_pre.astype(bf16)
    grad_hidden = grad_two + group_scatter(
        jnp.dot(grad_pre_low, w_up, preferred_element_type=f32)
    )
    grad_down = lax.psum_scatter(
        contract_rows(act_rows, grad_two_rows).astype(bf16), "dp", scatter_dimension=0, tiled=True
    )
    grad_up = lax.psum_scatter(
        contract_rows(grad_pre_low, hidden_rows).astype(bf16),
        "dp",
        scatter_dimension=0,
        tiled=True,
    )
    grad_one, grad_gain_one, grad_shift_one = norm_backward(
        grad_hidden, vector_rows[1], normed_one, scale_one
    )
    grad_out_bias = jnp.sum(grad_one, axis=0)
    grad_one_rows = group_gather(grad_one.astype(bf16))
    grad_att_low = contract_cols(grad_one_rows, w_out).astype(bf16)
    grad_att_low = grad_att_low.reshape(seq_count, SEQ, heads_local, HD)
    soft_again = jnp.exp(scores - log_total)
    grad_soft = jnp.einsum("sqhd,skhd->shqk", grad_att_low, value_rows, preferred_element_type=f32)
    grad_values = jnp.einsum(
        "shqk,sqhd->skhd", soft_again.astype(bf16), grad_att_low, preferred_element_type=f32
    )
    row_dot = jnp.sum(soft_again * grad_soft, axis=-1, keepdims=True)
    grad_scores = (soft_again * (grad_soft - row_dot)).astype(bf16)
    grad_queries = (
        jnp.einsum("shqk,skhd->sqhd", grad_scores, key_rows, preferred_element_type=f32)
        * score_scale
    )
    grad_keys = (
        jnp.einsum("shqk,sqhd->skhd", grad_scores, queries, preferred_element_type=f32)
        * score_scale
    )
    grad_qkv = jnp.stack((grad_queries, grad_keys, grad_values), axis=3).reshape(tok_count, -1)
    grad_qkv_bias = jnp.sum(grad_qkv, axis=0)
    grad_qkv_low = grad_qkv.astype(bf16)
    grad_qkv_weight = lax.psum_scatter(
        contract_rows(token_rows, grad_qkv_low)
        .astype(bf16)
        .reshape(n_col, n_dp, qkv_rows, width)
        .transpose(1, 0, 2, 3)
        .reshape(D, width),
        "dp",
        scatter_dimension=0,
        tiled=True,
    ).reshape(n_col, qkv_rows, width)
    input_grad = lax.dynamic_slice_in_dim(
        grad_one_rows, at_group * tokens.shape[1], tokens.shape[1], 1
    ).astype(f32) + feature_scatter(contract_cols(grad_qkv_low, w_qkv))
    grad_out = lax.psum_scatter(
        lax.all_to_all(
            contract_rows(attended, grad_one_rows).astype(bf16), "col", 1, 0, tiled=True
        ),
        "dp",
        scatter_dimension=0,
        tiled=True,
    )
    grad_vectors = jnp.stack(
        (
            grad_out_bias,
            grad_gain_one,
            grad_shift_one,
            grad_down_bias,
            grad_gain_two,
            grad_shift_two,
        ),
        axis=0,
    )
    ub_place = lax.dynamic_update_slice(
        jnp.zeros((n_row, n_dp, n_col, ff_own), f32),
        grad_up_bias.reshape(1, n_dp, 1, ff_own),
        (at_row, 0, at_col, 0),
    )
    sums = lax.psum(jnp.concatenate((grad_vectors.reshape(-1), ub_place.reshape(-1))), ("col", "row", "dp"))
    grad_vectors = lax.dynamic_slice_in_dim(
        sums[: 6 * D].reshape(6, D), (at_group * n_dp + at_dp) * n_vec, n_vec, 1
    )
    grad_up_bias = lax.dynamic_slice_in_dim(
        sums[6 * D :],
        ((at_row * n_col + at_col) * n_dp + at_dp) * up_bias.shape[0],
        up_bias.shape[0],
        0,
    )
    grad_qkv_bias = lax.dynamic_slice_in_dim(
        lax.psum(grad_qkv_bias, "dp").reshape(heads_local, -1),
        at_dp * qkv_bias.shape[1],
        qkv_bias.shape[1],
        1,
    )
    gradients = (
        lax.all_to_all(grad_qkv_weight, "col", 0, 2, tiled=True)
        .reshape(qkv_weight.shape)
        .astype(f32),
        grad_out.astype(f32),
        lax.all_to_all(grad_up, "col", 1, 0, tiled=True).T.astype(f32),
        lax.all_to_all(grad_down, "col", 1, 0, tiled=True).astype(f32),
        grad_qkv_bias,
        grad_up_bias,
        grad_vectors,
    )
    correct_one = 1.0 - BETA_ONE**STEP
    correct_two = 1.0 - BETA_TWO**STEP
    results = []
    for master, first_old, second_old, gradient, step_rate, decay_rate in zip(
        masters, firsts, seconds, gradients, RATES, DECAYS
    ):
        new_first = BETA_ONE * first_old + (1.0 - BETA_ONE) * gradient
        new_second = BETA_TWO * second_old + (1.0 - BETA_TWO) * gradient * gradient
        direction = new_first / correct_one / (jnp.sqrt(new_second / correct_two) + EPS_ADAM)
        results.append(master - step_rate * (direction + decay_rate * master))
        results.append(new_first)
        results.append(new_second)
    return (block_out, input_grad) + tuple(results)


def solution(mesh):
    placed = (
        P("dp", ("col", "row")),
        P("dp"),
        P("dp", ("col", "row")),
        P(("col", "dp"), "row", None, None),
        P(("col", "dp"), "row", None, None),
        P(("col", "dp"), "row", None, None),
        P(("row", "dp"), "col"),
        P(("row", "dp"), "col"),
        P(("row", "dp"), "col"),
        P("col", ("row", "dp")),
        P("col", ("row", "dp")),
        P("col", ("row", "dp")),
        P(("row", "dp"), "col"),
        P(("row", "dp"), "col"),
        P(("row", "dp"), "col"),
        P(("row", "col"), "dp"),
        P(("row", "col"), "dp"),
        P(("row", "col"), "dp"),
        P(("row", "col", "dp")),
        P(("row", "col", "dp")),
        P(("row", "col", "dp")),
        P(None, ("col", "row", "dp")),
        P(None, ("col", "row", "dp")),
        P(None, ("col", "row", "dp")),
    )
    return jax.shard_map(
        shards,
        mesh=mesh,
        in_specs=placed,
        out_specs=(
            P("dp", ("col", "row")),
            P("dp", ("col", "row")),
            P(("col", "dp"), "row", None, None),
            P(("col", "dp"), "row", None, None),
            P(("col", "dp"), "row", None, None),
            P(("row", "dp"), "col"),
            P(("row", "dp"), "col"),
            P(("row", "dp"), "col"),
            P("col", ("row", "dp")),
            P("col", ("row", "dp")),
            P("col", ("row", "dp")),
            P(("row", "dp"), "col"),
            P(("row", "dp"), "col"),
            P(("row", "dp"), "col"),
            P(("row", "col"), "dp"),
            P(("row", "col"), "dp"),
            P(("row", "col"), "dp"),
            P(("row", "col", "dp")),
            P(("row", "col", "dp")),
            P(("row", "col", "dp")),
            P(None, ("col", "row", "dp")),
            P(None, ("col", "row", "dp")),
            P(None, ("col", "row", "dp")),
        ),
        check_vma=False,
    )
```

```python
import math

import jax
import jax.numpy as jnp
from jax import lax
from jax.sharding import PartitionSpec as P

D = 1024
HD = 64
SEQ = 512
STEP = 10


EPS_NORM = 1e-05
BETA_ONE = 0.9
BETA_TWO = 0.999
EPS_ADAM = 1e-08
NEG_FILL = -1000000000.0
RATES = (0.05, 0.4, 0.05, 0.05, 0.3, 0.3, 0.5)
DECAYS = (0.01, 0.01, 0.01, 0.01, 0.0, 0.0, 0.0)


GROUP = ("col", "row")


def group_gather(block):
    return lax.all_gather(block, GROUP, axis=0, tiled=True)


def feature_gather(block):
    return lax.all_gather(block, GROUP, axis=1, tiled=True)


def group_scatter(partial_terms):
    return lax.psum_scatter(
        partial_terms.astype(jnp.bfloat16), GROUP, scatter_dimension=0, tiled=True
    ).astype(jnp.float32)


def feature_scatter(partial_terms):
    return lax.psum_scatter(
        partial_terms.astype(jnp.bfloat16), GROUP, scatter_dimension=1, tiled=True
    ).astype(jnp.float32)


def to_tokens(block):
    return lax.all_to_all(block, GROUP, split_axis=0, concat_axis=1, tiled=True)


def to_features(block):
    return lax.all_to_all(block, GROUP, split_axis=1, concat_axis=0, tiled=True)


def contract_rows(left_side, right_side):
    return lax.dot_general(
        left_side, right_side, (((0,), (0,)), ((), ())), preferred_element_type=jnp.float32
    )


def contract_cols(left_side, right_side):
    return lax.dot_general(
        left_side, right_side, (((1,), (1,)), ((), ())), preferred_element_type=jnp.float32
    )


def gelu_exact(values_in):
    return jax.nn.gelu(values_in, approximate=False)


def norm_forward(residual, norm_gain, norm_shift):
    mean_row = jnp.sum(residual, axis=1, keepdims=True) / D
    square_row = jnp.sum(residual * residual, axis=1, keepdims=True) / D
    scale_row = lax.rsqrt(square_row - mean_row * mean_row + EPS_NORM)
    normed = (residual - mean_row) * scale_row
    return (normed * norm_gain + norm_shift, normed, scale_row)


def norm_backward(grad_out, norm_gain, normed, scale_row):
    grad_normed = grad_out * norm_gain
    sum_plain = jnp.sum(grad_normed, axis=1, keepdims=True)
    sum_cross = jnp.sum(grad_normed * normed, axis=1, keepdims=True)
    grad_resid = scale_row * (grad_normed - sum_plain / D - normed * (sum_cross / D))
    return (grad_resid, jnp.sum(grad_out * normed, axis=0), jnp.sum(grad_out, axis=0))


def masked_scores(queries, key_rows, same_doc):
    raw_scores = jnp.einsum(
        "sqhd,skhd->shqk", queries, key_rows, preferred_element_type=jnp.float32
    ) * (1.0 / math.sqrt(HD))
    return jnp.where(same_doc, raw_scores, NEG_FILL)


def shards(
    tokens,
    segment_ids,
    out_grad,
    qkv_weight,
    qkv_first,
    qkv_second,
    out_weight,
    out_first,
    out_second,
    up_weight,
    up_first,
    up_second,
    down_weight,
    down_first,
    down_second,
    qkv_bias,
    qkv_bias_first,
    qkv_bias_second,
    up_bias,
    up_bias_first,
    up_bias_second,
    norm_vectors,
    norm_first,
    norm_second,
):
    masters = (qkv_weight, out_weight, up_weight, down_weight, qkv_bias, up_bias, norm_vectors)
    firsts = (qkv_first, out_first, up_first, down_first, qkv_bias_first, up_bias_first, norm_first)
    seconds = (
        qkv_second,
        out_second,
        up_second,
        down_second,
        qkv_bias_second,
        up_bias_second,
        norm_second,
    )
    bf16 = jnp.bfloat16
    f32 = jnp.float32
    n_dp, n_row, n_col = (lax.axis_size(name) for name in ("dp", "row", "col"))
    at_dp, at_row, at_col = (lax.axis_index(name) for name in ("dp", "row", "col"))
    at_group = at_col * n_row + at_row
    tok_count = tokens.shape[0]
    own_tok = tok_count // (n_row * n_col)
    seq_count = tok_count // SEQ
    score_scale = 1.0 / math.sqrt(HD)
    qkv_rows, heads_row = qkv_weight.shape[:2]
    heads_local = heads_row // n_col
    width = heads_local * 3 * HD
    feats = heads_local * HD
    d_col = D // n_col
    ff_own = up_weight.shape[1] // n_col
    ff_local = ff_own * n_dp
    w_qkv = (
        lax.all_gather(
            lax.all_to_all(
                qkv_weight.astype(bf16).reshape(qkv_rows, n_col, width), "col", 1, 0, tiled=True
            ).reshape(n_col * qkv_rows, width),
            "dp",
            axis=0,
            tiled=True,
        )
        .reshape(n_dp, n_col, qkv_rows, width)
        .transpose(1, 0, 2, 3)
        .reshape(D, width)
    )
    w_out = (
        lax.all_to_all(
            lax.all_gather(out_weight.astype(bf16), "dp", axis=0, tiled=True).reshape(
                n_col, feats, d_col
            ),
            "col",
            0,
            2,
            tiled=True,
        )
    ).reshape(feats, D)
    w_up = lax.all_gather(
        lax.all_to_all(up_weight.astype(bf16).T, "col", 0, 1, tiled=True), "dp", axis=0, tiled=True
    )
    w_down = lax.all_gather(
        lax.all_to_all(down_weight.astype(bf16), "col", 0, 1, tiled=True), "dp", axis=0, tiled=True
    )
    n_vec = norm_vectors.shape[1]
    small = lax.all_gather(
        jnp.concatenate(
            (norm_vectors.reshape(-1), qkv_bias.reshape(-1), up_bias.reshape(-1))
        ).astype(bf16),
        ("col", "row", "dp"),
        axis=0,
    ).astype(f32)
    vec_size, qb_size = norm_vectors.size, qkv_bias.size
    vector_rows = (
        small[:, :vec_size].reshape(-1, 6, n_vec).transpose(1, 0, 2).reshape(6, D)
    )
    small_group = small.reshape(n_col, n_row, n_dp, -1)
    qb_all = lax.dynamic_index_in_dim(
        small_group[..., vec_size : vec_size + qb_size].reshape(n_col * n_row, n_dp, -1),
        at_group,
        0,
        keepdims=False,
    )
    b_qkv = qb_all.reshape(n_dp, heads_local, -1).transpose(1, 0, 2).reshape(-1)
    ub_all = lax.dynamic_index_in_dim(
        small_group[..., vec_size + qb_size :], at_row, 1, keepdims=False
    ).reshape(n_dp, n_col, ff_own)
    b_up = lax.dynamic_index_in_dim(ub_all, at_col, 1, keepdims=False).reshape(-1)

    seg_rows = segment_ids.reshape(seq_count, SEQ)
    same_doc = seg_rows[:, None, :, None] == seg_rows[:, None, None, :]
    token_rows = feature_gather(tokens)
    own_tokens = lax.dynamic_slice_in_dim(token_rows, at_group * own_tok, own_tok, 0)
    own_out_grad = to_tokens(out_grad).astype(f32)
    qkv_local = jnp.dot(token_rows, w_qkv, preferred_element_type=f32) + b_qkv
    qkv_low = qkv_local.astype(bf16).reshape(seq_count, SEQ, heads_local, 3, HD)
    queries = qkv_low[:, :, :, 0]
    key_rows = qkv_low[:, :, :, 1]
    value_rows = qkv_low[:, :, :, 2]
    scores = masked_scores(queries, key_rows, same_doc)
    row_peak = jnp.max(scores, axis=-1, keepdims=True)
    exp_scores = jnp.exp(scores - row_peak)
    row_total = jnp.sum(exp_scores, axis=-1, keepdims=True)
    log_total = row_peak + jnp.log(row_total)
    soft_low = (exp_scores / row_total).astype(bf16)
    attended = (
        jnp.einsum("shqk,skhd->sqhd", soft_low, value_rows, preferred_element_type=f32)
        .reshape(tok_count, feats)
        .astype(bf16)
    )
    residual_one = (
        own_tokens.astype(f32)
        + group_scatter(jnp.dot(attended, w_out, preferred_element_type=f32))
        + vector_rows[0]
    )
    hidden_one, normed_one, scale_one = norm_forward(residual_one, vector_rows[1], vector_rows[2])
    hidden_rows = group_gather(hidden_one.astype(bf16))
    pre_act = contract_cols(hidden_rows, w_up) + b_up
    act_rows = gelu_exact(pre_act).astype(bf16)
    residual_two = (
        hidden_one
        + group_scatter(jnp.dot(act_rows, w_down, preferred_element_type=f32))
        + vector_rows[3]
    )
    output_rows, normed_two, scale_two = norm_forward(residual_two, vector_rows[4], vector_rows[5])
    block_out = to_features(output_rows.astype(bf16))
    grad_two, grad_gain_two, grad_shift_two = norm_backward(
        own_out_grad, vector_rows[4], normed_two, scale_two
    )
    grad_down_bias = jnp.sum(grad_two, axis=0)
    grad_two_rows = group_gather(grad_two.astype(bf16))
    grad_act = contract_cols(grad_two_rows, w_down)
    gelu_value, gelu_pull = jax.vjp(gelu_exact, pre_act)
    grad_pre = gelu_pull(grad_act)[0]
    grad_up_bias = jnp.sum(grad_pre, axis=0)
    grad_pre_low = grad_pre.astype(bf16)
    grad_hidden = grad_two + group_scatter(
        jnp.dot(grad_pre_low, w_up, preferred_element_type=f32)
    )
    grad_down = lax.psum_scatter(
        contract_rows(act_rows, grad_two_rows).astype(bf16), "dp", scatter_dimension=0, tiled=True
    )
    grad_up = lax.psum_scatter(
        contract_rows(grad_pre_low, hidden_rows).astype(bf16),
        "dp",
        scatter_dimension=0,
        tiled=True,
    )
    grad_one, grad_gain_one, grad_shift_one = norm_backward(
        grad_hidden, vector_rows[1], normed_one, scale_one
    )
    grad_out_bias = jnp.sum(grad_one, axis=0)
    grad_one_rows = group_gather(grad_one.astype(bf16))
    grad_att_low = contract_cols(grad_one_rows, w_out).astype(bf16)
    grad_att_low = grad_att_low.reshape(seq_count, SEQ, heads_local, HD)
    soft_again = jnp.exp(scores - log_total)
    grad_soft = jnp.einsum("sqhd,skhd->shqk", grad_att_low, value_rows, preferred_element_type=f32)
    grad_values = jnp.einsum(
        "shqk,sqhd->skhd", soft_again.astype(bf16), grad_att_low, preferred_element_type=f32
    )
    row_dot = jnp.sum(soft_again * grad_soft, axis=-1, keepdims=True)
    grad_scores = (soft_again * (grad_soft - row_dot)).astype(bf16)
    grad_queries = (
        jnp.einsum("shqk,skhd->sqhd", grad_scores, key_rows, preferred_element_type=f32)
        * score_scale
    )
    grad_keys = (
        jnp.einsum("shqk,sqhd->skhd", grad_scores, queries, preferred_element_type=f32)
        * score_scale
    )
    grad_qkv = jnp.stack((grad_queries, grad_keys, grad_values), axis=3).reshape(tok_count, -1)
    grad_qkv_bias = jnp.sum(grad_qkv, axis=0)
    grad_qkv_low = grad_qkv.astype(bf16)
    grad_qkv_weight = lax.psum_scatter(
        contract_rows(token_rows, grad_qkv_low)
        .astype(bf16)
        .reshape(n_col, n_dp, qkv_rows, width)
        .transpose(1, 0, 2, 3)
        .reshape(D, width),
        "dp",
        scatter_dimension=0,
        tiled=True,
    ).reshape(n_col, qkv_rows, width)
    input_grad = lax.dynamic_slice_in_dim(
        grad_one_rows, at_group * tokens.shape[1], tokens.shape[1], 1
    ).astype(f32) + feature_scatter(contract_cols(grad_qkv_low, w_qkv))
    grad_out = lax.psum_scatter(
        lax.all_to_all(
            contract_rows(attended, grad_one_rows).astype(bf16), "col", 1, 0, tiled=True
        ),
        "dp",
        scatter_dimension=0,
        tiled=True,
    )
    grad_vectors = jnp.stack(
        (
            grad_out_bias,
            grad_gain_one,
            grad_shift_one,
            grad_down_bias,
            grad_gain_two,
            grad_shift_two,
        ),
        axis=0,
    )
    ub_place = lax.dynamic_update_slice(
        jnp.zeros((n_row, n_dp, n_col, ff_own), f32),
        grad_up_bias.reshape(1, n_dp, 1, ff_own),
        (at_row, 0, at_col, 0),
    )
    ub_blocks = (
        ub_place.reshape(n_row, n_col, n_dp, -1).transpose(1, 0, 2, 3).reshape(-1, up_bias.shape[0])
    )
    qb_blocks = lax.dynamic_update_slice(
        jnp.zeros((n_col * n_row, n_dp, qb_size), f32),
        grad_qkv_bias.reshape(heads_local, n_dp, -1).transpose(1, 0, 2).reshape(1, n_dp, qb_size),
        (at_group, 0, 0),
    ).reshape(-1, qb_size)
    vec_blocks = grad_vectors.reshape(6, -1, n_vec).transpose(1, 0, 2).reshape(-1, vec_size)
    sums = jnp.sum(
        lax.all_to_all(
            jnp.concatenate((vec_blocks, qb_blocks, ub_blocks), axis=1),
            ("col", "row", "dp"),
            0,
            0,
            tiled=True,
        ),
        axis=0,
    )
    grad_vectors = sums[:vec_size].reshape(norm_vectors.shape)
    grad_qkv_bias = sums[vec_size : vec_size + qb_size].reshape(qkv_bias.shape)
    grad_up_bias = sums[vec_size + qb_size :]
    gradients = (
        lax.all_to_all(grad_qkv_weight, "col", 0, 2, tiled=True)
        .reshape(qkv_weight.shape)
        .astype(f32),
        grad_out.astype(f32),
        lax.all_to_all(grad_up, "col", 1, 0, tiled=True).T.astype(f32),
        lax.all_to_all(grad_down, "col", 1, 0, tiled=True).astype(f32),
        grad_qkv_bias,
        grad_up_bias,
        grad_vectors,
    )
    correct_one = 1.0 - BETA_ONE**STEP
    correct_two = 1.0 - BETA_TWO**STEP
    results = []
    for master, first_old, second_old, gradient, step_rate, decay_rate in zip(
        masters, firsts, seconds, gradients, RATES, DECAYS
    ):
        new_first = BETA_ONE * first_old + (1.0 - BETA_ONE) * gradient
        new_second = BETA_TWO * second_old + (1.0 - BETA_TWO) * gradient * gradient
        direction = new_first / correct_one / (jnp.sqrt(new_second / correct_two) + EPS_ADAM)
        results.append(master - step_rate * (direction + decay_rate * master))
        results.append(new_first)
        results.append(new_second)
    return (block_out, input_grad) + tuple(results)


def solution(mesh):
    placed = (
        P("dp", ("col", "row")),
        P("dp"),
        P("dp", ("col", "row")),
        P(("col", "dp"), "row", None, None),
        P(("col", "dp"), "row", None, None),
        P(("col", "dp"), "row", None, None),
        P(("row", "dp"), "col"),
        P(("row", "dp"), "col"),
        P(("row", "dp"), "col"),
        P("col", ("row", "dp")),
        P("col", ("row", "dp")),
        P("col", ("row", "dp")),
        P(("row", "dp"), "col"),
        P(("row", "dp"), "col"),
        P(("row", "dp"), "col"),
        P(("row", "col"), "dp"),
        P(("row", "col"), "dp"),
        P(("row", "col"), "dp"),
        P(("row", "col", "dp")),
        P(("row", "col", "dp")),
        P(("row", "col", "dp")),
        P(None, ("col", "row", "dp")),
        P(None, ("col", "row", "dp")),
        P(None, ("col", "row", "dp")),
    )
    return jax.shard_map(
        shards,
        mesh=mesh,
        in_specs=placed,
        out_specs=(
            P("dp", ("col", "row")),
            P("dp", ("col", "row")),
            P(("col", "dp"), "row", None, None),
            P(("col", "dp"), "row", None, None),
            P(("col", "dp"), "row", None, None),
            P(("row", "dp"), "col"),
            P(("row", "dp"), "col"),
            P(("row", "dp"), "col"),
            P("col", ("row", "dp")),
            P("col", ("row", "dp")),
            P("col", ("row", "dp")),
            P(("row", "dp"), "col"),
            P(("row", "dp"), "col"),
            P(("row", "dp"), "col"),
            P(("row", "col"), "dp"),
            P(("row", "col"), "dp"),
            P(("row", "col"), "dp"),
            P(("row", "col", "dp")),
            P(("row", "col", "dp")),
            P(("row", "col", "dp")),
            P(None, ("col", "row", "dp")),
            P(None, ("col", "row", "dp")),
            P(None, ("col", "row", "dp")),
        ),
        check_vma=False,
    )
```
